32 devices in a mesh: ens: 2 (over y), ta: 4 (over z), gz: 2 (over x), gy: 2 (over core).
Axes of the slice: x: 2, y: 2, z: 4, core: 2. Of those that a mesh axis runs over, the one named last changes fastest.
Arguments:
- raw_links: float32 [8, 3, 3, 2, 8, 4, 256], P('ens', None, None, None, 'ta', 'gz', 'gy'), parts along dimension 0, may hold values from -0.25 to 1.25, as said below
Outputs:
- relaxed_links: float32 [8, 3, 3, 2, 8, 4, 256], P('ens', None, None, None, 'ta', 'gz', 'gy'), parts along dimension 0
The draws below stay inside these ranges and needn't reach their ends.
There are 2 independent parts, one for each index of `ens`. The reference program is written for one: setup_inputs(seed, part) draws one part's arguments, and reference() takes and returns one part's arrays. A program takes and returns all parts, laid end to end along the dimension named above; each array names one. Nothing has to cross between parts.
Inputs may be any that keep to these rules, and one draw needn't show every extreme that they name: `raw_links`: each real entry lies within 0.25 of the corresponding entry of the identity matrix.
All inputs are finite; a program needn't handle non-finite values.
Results may differ from the reference program's by a relative error of at most 0.0003.
Values sent between devices are 32-bit elements; how exact they have to be, the bound alone decides.
A program may use at most 64 MiB of HBM per device.

```python
import jax
import jax.numpy as jnp
from jax import lax

X = 16
SWEEPS = 1
NY = 16
NZ = 4
NT = 8


def draw_raw_links(key, part):
    key = jax.random.fold_in(key, 7)
    shape = (4, 3, 3, 2, NT, NZ, NY * X)
    noise = jnp.clip(0.08 * jax.random.normal(key, shape, jnp.float32), -0.25, 0.25)
    identity = jnp.eye(3, dtype=jnp.float32)[None, :, :, None, None, None, None] * jnp.array([1.0, 0.0], jnp.float32)[None, None, None, :, None, None, None]
    return identity + noise


def setup_inputs(seed: int = 0, part: int = 0) -> dict:
    splits = jax.random.split(jax.random.key(seed), 2)
    part_keys = jax.random.split(jax.random.fold_in(splits[1], part), 2)
    return {
        "raw_links": draw_raw_links(jax.random.fold_in(jax.random.fold_in(splits[1], part), 71), part),
    }


def complex_product(left, right):
    left_real, left_imag = (left[:, :, 0], left[:, :, 1])
    right_real, right_imag = (right[:, :, 0], right[:, :, 1])
    real_part = 0.0
    imag_part = 0.0
    for k in range(3):
        real_part = real_part + left_real[:, k][:, None] * right_real[k][None] - left_imag[:, k][:, None] * right_imag[k][None]
        imag_part = imag_part + left_real[:, k][:, None] * right_imag[k][None] + left_imag[:, k][:, None] * right_real[k][None]
    return jnp.stack([real_part, imag_part], axis=2)

def dagger(matrix):
    return jnp.stack([jnp.swapaxes(matrix[:, :, 0], 0, 1), -jnp.swapaxes(matrix[:, :, 1], 0, 1)], axis=2)

def third_row(leading, second):
    entries = []
    for j in range(3):
        k = (j + 1) % 3
        m = (j + 2) % 3
        real_part = leading[:, k, 0] * second[:, m, 0] - leading[:, k, 1] * second[:, m, 1] - (leading[:, m, 0] * second[:, k, 0] - leading[:, m, 1] * second[:, k, 1])
        imag_part = leading[:, k, 0] * second[:, m, 1] + leading[:, k, 1] * second[:, m, 0] - (leading[:, m, 0] * second[:, k, 1] + leading[:, m, 1] * second[:, k, 0])
        entries.append(jnp.stack([real_part, -imag_part], axis=1))
    return jnp.stack(entries, axis=1)

def unitarize(raw_matrix):
    leading = raw_matrix[:, 0]
    second = raw_matrix[:, 1]
    leading = leading / jnp.sqrt(lax.optimization_barrier(jnp.sum(leading * leading, axis=(1, 2), keepdims=True)))
    correlation_real = lax.optimization_barrier(jnp.sum(leading[:, :, 0] * second[:, :, 0] + leading[:, :, 1] * second[:, :, 1], axis=1))
    correlation_imag = lax.optimization_barrier(jnp.sum(leading[:, :, 0] * second[:, :, 1] - leading[:, :, 1] * second[:, :, 0], axis=1))
    second_real = second[:, :, 0] - (correlation_real[:, None] * leading[:, :, 0] - correlation_imag[:, None] * leading[:, :, 1])
    second_imag = second[:, :, 1] - (correlation_real[:, None] * leading[:, :, 1] + correlation_imag[:, None] * leading[:, :, 0])
    second = jnp.stack([second_real, second_imag], axis=2)
    second = second / jnp.sqrt(lax.optimization_barrier(jnp.sum(second * second, axis=(1, 2), keepdims=True)))
    return jnp.stack([leading, second, third_row(leading, second)], axis=1)

def unit_step(direction, sign):
    return tuple((sign if i == direction else 0 for i in range(4)))

def staple_sum(fetch, direction):
    staple_total = None
    still = (0, 0, 0, 0)
    for other in range(4):
        if other == direction:
            continue
        step_mu = unit_step(direction, 1)
        step_nu = unit_step(other, 1)
        back_nu = unit_step(other, -1)
        across = tuple((step_mu[i] - step_nu[i] for i in range(4)))
        upper_loop = complex_product(complex_product(fetch(other, step_mu), dagger(fetch(direction, step_nu))), dagger(fetch(other, still)))
        lower_loop = complex_product(complex_product(dagger(fetch(other, across)), dagger(fetch(direction, back_nu))), fetch(other, back_nu))
        if staple_total is None:
            staple_total = upper_loop + lower_loop
        else:
            staple_total = staple_total + upper_loop + lower_loop
    return staple_total

def times_row(coef_real, coef_imag, row_data):
    return jnp.stack([coef_real * row_data[:, 0] - coef_imag * row_data[:, 1], coef_real * row_data[:, 1] + coef_imag * row_data[:, 0]], axis=1)

def rotate_rows(matrix, a, b, mixing):
    row_a = matrix[a]
    row_b = matrix[b]
    new_a = times_row(mixing[0], mixing[1], row_a) + times_row(mixing[2], mixing[3], row_b)
    new_b = times_row(mixing[4], mixing[5], row_a) + times_row(mixing[6], mixing[7], row_b)
    return matrix.at[a].set(new_a).at[b].set(new_b)

def overrelax(link_now, staple):
    product = complex_product(link_now, staple)
    for a, b in ((0, 1), (0, 2), (1, 2)):
        quat_zero = 0.5 * (product[a, a, 0] + product[b, b, 0])
        quat_one = 0.5 * (product[a, b, 1] + product[b, a, 1])
        quat_two = 0.5 * (product[a, b, 0] - product[b, a, 0])
        quat_three = 0.5 * (product[a, a, 1] - product[b, b, 1])
        vector_sq = quat_one * quat_one + quat_two * quat_two + quat_three * quat_three
        length_sq = quat_zero * quat_zero + vector_sq
        coef_zero = (quat_zero * quat_zero - vector_sq) / length_sq
        coef_one = -2.0 * quat_zero * quat_one / length_sq
        coef_two = -2.0 * quat_zero * quat_two / length_sq
        coef_three = -2.0 * quat_zero * quat_three / length_sq
        mixing = (coef_zero, coef_three, coef_two, coef_one, -coef_two, coef_one, coef_zero, -coef_three)
        link_now = rotate_rows(link_now, a, b, mixing)
        product = rotate_rows(product, a, b, mixing)
    return link_now

def reference(raw_links):
    gauge_links = unitarize(raw_links)
    lattice = gauge_links.reshape(gauge_links.shape[:6] + (NY, X))
    t_pos = jnp.arange(NT, dtype=jnp.int32)[:, None, None, None]
    z_pos = jnp.arange(NZ, dtype=jnp.int32)[None, :, None, None]
    y_pos = jnp.arange(NY, dtype=jnp.int32)[None, None, :, None]
    x_pos = jnp.arange(X, dtype=jnp.int32)[None, None, None, :]
    checker = (t_pos + z_pos + y_pos + x_pos) % 2
    for sweep_index in range(SWEEPS):
        for direction in range(4):
            for parity_bit in range(2):
                current = lattice

                def fetch(d, offsets):
                    field_data = current[d]
                    for i in range(4):
                        if offsets[i] != 0:
                            field_data = jnp.roll(field_data, -offsets[i], axis=3 + i)
                    return field_data
                staple = staple_sum(fetch, direction)
                renewed = overrelax(current[direction], staple)
                lattice = current.at[direction].set(jnp.where(checker == parity_bit, renewed, current[direction]))
    return lattice.reshape(raw_links.shape)
```

```python
import functools

import jax
import jax.numpy as jnp
from jax import lax
from jax.experimental import pallas as pl
from jax.experimental.pallas import tpu as pltpu
from jax.sharding import PartitionSpec as P

X = 16
LANES = 128
MESH = pl.DeviceIdType.MESH


def product(a, b, a_dagger=False, b_dagger=False):
    depth = a[0].shape[0] if a_dagger else a[0].shape[1]
    real = imag = None
    for k in range(depth):
        left = [(part[k] if a_dagger else part[:, k])[:, None] for part in a]
        right = [(part[:, k] if b_dagger else part[k])[None] for part in b]
        if a_dagger != b_dagger:
            real_term = left[0] * right[0] + left[1] * right[1]
            if a_dagger:
                imag_term = left[0] * right[1] - left[1] * right[0]
            else:
                imag_term = left[1] * right[0] - left[0] * right[1]
        else:
            real_term = left[0] * right[0] - left[1] * right[1]
            imag_term = left[0] * right[1] + left[1] * right[0]
        real = real_term if real is None else real + real_term
        imag = imag_term if imag is None else imag + imag_term
    return real, imag


def third(real, imag):
    rows = []
    for j in range(3):
        k, m = (j + 1) % 3, (j + 2) % 3
        a_r, a_i, b_r, b_i = real[0, k], imag[0, k], real[1, m], imag[1, m]
        c_r, c_i, d_r, d_i = real[0, m], imag[0, m], real[1, k], imag[1, k]
        rows.append(
            (
                (a_r * b_r - a_i * b_i) - (c_r * d_r - c_i * d_i),
                (c_r * d_i + c_i * d_r) - (a_r * b_i + a_i * b_r),
            )
        )
    return jnp.stack([r for r, _ in rows]), jnp.stack([i for _, i in rows])


def closed(pair):
    real, imag = pair
    last_r, last_i = third(real, imag)
    return (
        jnp.concatenate([real, last_r[None]], axis=0),
        jnp.concatenate([imag, last_i[None]], axis=0),
    )


def two_rows(pair):
    return pair[0][:2], pair[1][:2]


def two_columns(pair):
    return pair[0][:, :2], pair[1][:, :2]


def plus(a, b):
    return a[0] + b[0], a[1] + b[1]


def roll(value, shift, axis):
    return pltpu.roll(value, shift % value.shape[axis], axis)


def project(rows):
    lead, second = rows[0], rows[1]
    square = lead * lead
    norm = square[0, 0] + square[0, 1] + square[1, 0] + square[1, 1] + square[2, 0] + square[2, 1]
    lead = lead * (1.0 / jnp.sqrt(norm))[None, None]
    cr = ci = None
    for j in range(3):
        r = lead[j, 0] * second[j, 0] + lead[j, 1] * second[j, 1]
        i = lead[j, 0] * second[j, 1] - lead[j, 1] * second[j, 0]
        cr = r if cr is None else cr + r
        ci = i if ci is None else ci + i
    new = []
    norm = None
    for j in range(3):
        r = second[j, 0] - (cr * lead[j, 0] - ci * lead[j, 1])
        i = second[j, 1] - (cr * lead[j, 1] + ci * lead[j, 0])
        new.append((r, i))
        norm = r * r + i * i if norm is None else norm + (r * r + i * i)
    inverse = 1.0 / jnp.sqrt(norm)
    lead = [(lead[j, 0], lead[j, 1]) for j in range(3)]
    return [lead, [(r * inverse, i * inverse) for r, i in new]]


def reflect(link, staple):
    w_r, w_i = product(link, staple)
    w = {(i, j): (w_r[i, j], w_i[i, j]) for i in range(3) for j in range(3)}
    u = {i: (link[0][i], link[1][i]) for i in range(3)}
    needed = {(0, 1): ((0, 1, 2), (1, 2)), (0, 2): ((), (1, 2)), (1, 2): ((), ())}
    for a, b in ((0, 1), (0, 2), (1, 2)):
        q0 = 0.5 * (w[a, a][0] + w[b, b][0])
        q1 = 0.5 * (w[a, b][1] + w[b, a][1])
        q2 = 0.5 * (w[a, b][0] - w[b, a][0])
        q3 = 0.5 * (w[a, a][1] - w[b, b][1])
        vector = q1 * q1 + q2 * q2 + q3 * q3
        square = q0 * q0
        inverse = 1.0 / (square + vector)
        c0 = (square - vector) * inverse
        scale = -2.0 * q0 * inverse
        c1, c2, c3 = scale * q1, scale * q2, scale * q3

        def first(top, low):
            return (
                (c0 * top[0] - c3 * top[1]) + (c2 * low[0] - c1 * low[1]),
                (c0 * top[1] + c3 * top[0]) + (c2 * low[1] + c1 * low[0]),
            )

        def last(top, low):
            return (
                (c0 * low[0] + c3 * low[1]) - (c2 * top[0] + c1 * top[1]),
                (c0 * low[1] - c3 * low[0]) + (c1 * top[0] - c2 * top[1]),
            )

        u[a], u[b] = first(u[a], u[b]), last(u[a], u[b])
        tops, lows = needed[a, b]
        new = {(a, j): first(w[a, j], w[b, j]) for j in tops}
        new.update({(b, j): last(w[a, j], w[b, j]) for j in lows})
        w.update(new)
    return jnp.stack([u[i][0] for i in range(3)]), jnp.stack([u[i][1] for i in range(3)])


def kernel(
    counts,
    x_ref,
    o_ref,
    raw,
    packed,
    gathered,
    rim,
    link_r,
    link_i,
    rim_r,
    rim_i,
    up_out,
    up_in,
    down_out,
    down_in,
    natural,
    load_sem,
    own_sem,
    sib_send,
    sib_recv,
    gz_send,
    gz_recv,
    fwd_send,
    fwd_recv,
    rim_send,
    rim_recv,
    rfw_send,
    rfw_recv,
    up_send,
    up_recv,
    down_send,
    down_recv,
    store_sem,
):
    ta_n, gz_n, t_len, z_len = counts
    piece = t_len * z_len
    rows = gz_n * piece
    ta, gz, gy = lax.axis_index("ta"), lax.axis_index("gz"), lax.axis_index("gy")
    later, earlier = lax.rem(ta + 1, ta_n), lax.rem(ta + ta_n - 1, ta_n)
    sibling = {"gy": 1 - gy}

    def side(k):
        return lax.rem(gz + k, gz_n)

    def behind(k):
        return lax.rem(gz + gz_n - k, gz_n)

    loads = []
    for half in range(2):
        for z in range(z_len):
            for t in range(t_len):
                row = half * piece + z * t_len + t
                loads.append(
                    pltpu.make_async_copy(
                        x_ref.at[2 * half : 2 * half + 2, 0:2, :, :, t, z, :],
                        raw.at[:, :, :, :, row, :],
                        load_sem.at[row],
                    )
                )
    for copy in loads:
        copy.start()

    barrier = pltpu.get_barrier_semaphore()
    greeted = [sibling] + [{"gz": side(k)} for k in range(1, gz_n)]
    for k in range(gz_n):
        greeted.append({"ta": later, "gz": side(k)})
        greeted.append({"ta": earlier, "gz": side(k)})
    for device in greeted:
        pl.semaphore_signal(barrier, inc=1, device_id=device, device_id_type=MESH)

    for copy in loads:
        copy.wait()

    small = (2 * piece, LANES)
    row_id = lax.broadcasted_iota(jnp.int32, small, 0)
    lane_id = lax.broadcasted_iota(jnp.int32, small, 1)
    inner = row_id % piece
    place = lane_id % 64
    odd = (inner // t_len + inner % t_len + place // 8 + lane_id // 64) % 2
    pick = (place // 8) * X + 2 * (place % 8) + odd
    for pair in range(2):
        for i, row in enumerate(project(raw[pair])):
            for j, entry in enumerate(row):
                for c in range(2):
                    packed[pair, i, j, c] = jnp.take_along_axis(entry[c], pick, axis=1)

    pl.semaphore_wait(barrier, len(greeted))

    def block(d):
        return packed.at[d % 2, :, :, :, pl.ds((d // 2) * piece, piece), :]

    def slot(core, d, where):
        return gathered.at[core, d, :, :, :, pl.ds(where * piece, piece), :]

    def remote(src, dst, send, recv, device):
        return pltpu.make_async_remote_copy(
            src_ref=src, dst_ref=dst, send_sem=send, recv_sem=recv, device_id=device, device_id_type=MESH
        )

    sends = []
    order = (0, 1, 2, 3)
    own, near, sent = {}, {}, {}
    for d in order:
        for k in range(1, gz_n):
            sent[d, k] = remote(
                block(d), slot(gy, d, gz), gz_send.at[k - 1, d], gz_recv.at[k - 1, d], {"gz": side(k)}
            )
            sent[d, k].start()
    edge = {}
    for k in range(gz_n):
        for z in range(z_len):
            for d in range(1, 4):
                row = (d // 2) * piece + z * t_len
                to = (gz * z_len + z) * t_len + t_len - 1
                edge[k, z, d] = remote(
                    packed.at[d % 2, :, :, :, row, :],
                    rim.at[gy, d - 1, :, :, :, to, :],
                    rim_send.at[k, z, d - 1],
                    rim_recv.at[k, z, d - 1],
                    {"ta": earlier, "gz": side(k)},
                )
                edge[k, z, d].start()
    for d in order:
        near[d] = remote(block(d), slot(gy, d, gz), sib_send.at[d], sib_recv.at[d], sibling)
        near[d].start()
        own[d] = pltpu.make_async_copy(block(d), slot(gy, d, gz), own_sem.at[d])
        own[d].start()
    passed = []
    for d in order:
        for k in range(1, gz_n):
            sent[d, k].wait_recv()
            region = slot(gy, d, behind(k))
            copy = remote(region, region, fwd_send.at[k - 1, d], fwd_recv.at[k - 1, d], sibling)
            copy.start()
            passed.append(copy)
    for k in range(gz_n):
        for z in range(z_len):
            for d in range(1, 4):
                edge[k, z, d].wait_recv()
                to = (behind(k) * z_len + z) * t_len + t_len - 1
                region = rim.at[gy, d - 1, :, :, :, to, :]
                copy = remote(region, region, rfw_send.at[k, z, d - 1], rfw_recv.at[k, z, d - 1], sibling)
                copy.start()
                passed.append(copy)
    for d in order:
        own[d].wait()
        near[d].wait()
        for k in range(1, gz_n):
            sent[d, k].wait_send()
    for copy in edge.values():
        copy.wait_send()
    for copy in passed:
        copy.wait()

    full = (rows, LANES)
    row_id = lax.broadcasted_iota(jnp.int32, full, 0)
    lane_id = lax.broadcasted_iota(jnp.int32, full, 1)
    t_pos = row_id % t_len
    first_t, last_t = t_pos == 0, t_pos == t_len - 1
    low = lane_id < 64
    shade = (row_id // t_len + t_pos + lane_id // 8) % 2
    even_x = (shade == 0, shade == 1)
    x_first, x_last = lane_id % 8 == 0, lane_id % 8 == 7

    def choose(mask, a, b):
        shape = a.shape
        return jnp.where(jnp.broadcast_to(mask, shape), a, b)

    def spread(piece_0, piece_1, put):
        for parity in range(2):
            if parity == 0:
                value = choose(low, piece_0, roll(piece_1, 64, 4))
            else:
                value = choose(low, roll(piece_0, 64, 4), piece_1)
            put(parity, closed((value[:, :, 0], value[:, :, 1])))

    for d in range(4):

        def put(parity, pair):
            link_r[parity, d], link_i[parity, d] = pair

        spread(gathered[0, d], gathered[1, d], put)
    for d in range(3):

        def put(parity, pair):
            rim_r[parity, d], rim_i[parity, d] = pair

        spread(rim[0, d], rim[1, d], put)

    def link(d, parity):
        return link_r[parity, d], link_i[parity, d]

    def rim_link(d, parity):
        return rim_r[parity, d - 1], rim_i[parity, d - 1]

    def moved(value, direction, sign, parity):
        sub, lane = value.ndim - 2, value.ndim - 1
        if direction == 0:
            return roll(value, -sign, sub)
        if direction == 1:
            return roll(value, -sign * t_len, sub)
        if direction == 2:
            return roll(value, -sign * 8, lane)
        edge_x = x_last if sign > 0 else x_first
        turned = choose(edge_x, roll(value, sign * 7, lane), roll(value, -sign, lane))
        stays = even_x[parity] if sign > 0 else even_x[1 - parity]
        return choose(stays, value, turned)

    def shifted(pair, direction, sign, parity, beyond=None):
        out = []
        for n in range(2):
            value = moved(pair[n], direction, sign, parity)
            if direction == 0:
                value = choose(last_t if sign > 0 else first_t, beyond[n], value)
            out.append(value)
        return tuple(out)

    def ahead(nu, mu, parity, cut):
        beyond = cut(rim_link(nu, 1 - parity)) if mu == 0 else None
        return shifted(cut(link(nu, 1 - parity)), mu, 1, parity, beyond)

    def upper(mu, nu, parity, beyond=None):
        if nu == 0:
            across = closed(shifted(two_rows(link(mu, 1 - parity)), 0, 1, parity, beyond))
        else:
            across = shifted(link(mu, 1 - parity), nu, 1, parity)
        part = product(ahead(nu, mu, parity, two_rows), across, b_dagger=True)
        return product(part, link(nu, parity), b_dagger=True)

    def lower(mu, nu, parity):
        part = product(link(mu, parity), ahead(nu, mu, parity, two_columns))
        return product(part, link(nu, parity), a_dagger=True)

    def both(mu, nu, parity):
        up = closed(upper(mu, nu, parity))
        down = closed(shifted(lower(mu, nu, 1 - parity), nu, -1, parity))
        return plus(up, down)

    def renew(mu, parity, staple):
        link_r[parity, mu], link_i[parity, mu] = reflect(link(mu, parity), staple)

    messages = []

    def send_up(n, pair):
        up_out[n] = choose(first_t, roll(pair[0], -1, 2), pair[1])
        copy = remote(up_out.at[n], up_in.at[n], up_send.at[n], up_recv.at[n], {"ta": later})
        copy.start()
        messages.append(copy)
        return copy

    def send_down(n, pair):
        down_out[n] = choose(first_t, pair[0], roll(pair[1], 1, 2))
        copy = remote(down_out.at[n], down_in.at[n], down_send.at[n], down_recv.at[n], {"ta": earlier})
        copy.start()
        messages.append(copy)
        return copy

    stores = []
    row_natural = (row_id // t_len + t_pos + lane_id // X + lane_id % X) % 2
    back = (lane_id // X) * 8 + (lane_id % X) // 2 + 64 * row_natural

    def write(d):
        for i in range(3):
            for j in range(3):
                for c, ref in enumerate((link_r, link_i)):
                    zero = jnp.where(gy == 0, ref[0, d, i, j], roll(ref[0, d, i, j], 64, 1))
                    one = jnp.where(gy == 0, roll(ref[1, d, i, j], 64, 1), ref[1, d, i, j])
                    natural[d, i, j, c] = jnp.take_along_axis(jnp.where(low, zero, one), back, axis=1)
        for z in range(z_len):
            for t in range(t_len):
                copy = pltpu.make_async_copy(
                    natural.at[d, :, :, :, gz * piece + z * t_len + t, :],
                    o_ref.at[d, :, :, :, t, z, :],
                    store_sem.at[d, z * t_len + t],
                )
                copy.start()
                stores.append(copy)

    for parity in range(2):
        total = both(0, 1, parity)
        for nu in (2, 3):
            total = plus(total, both(0, nu, parity))
        renew(0, parity, total)

    back_loop, from_below = {}, {}
    for mu in (1, 2, 3):
        back_loop[mu] = lower(mu, 0, 1)
        from_below[mu] = send_up(mu - 1, back_loop[mu])
    write(0)

    def arrived(n):
        value = up_in[n]
        return value, roll(value, -1, 2)

    def time_part(mu, parity, ahead_rows, behind_loop, n):
        up = closed(upper(mu, 0, parity, ahead_rows))
        down = closed(shifted(behind_loop, 0, -1, parity, arrived(n)))
        return plus(up, down)

    for mu in (1, 2, 3):
        others = [nu for nu in (1, 2, 3) if nu != mu]
        total = plus(both(mu, others[0], 0), both(mu, others[1], 0))
        from_below[mu].wait_recv()
        total = plus(total, time_part(mu, 0, two_rows(rim_link(mu, 1)), back_loop[mu], mu - 1))
        renew(mu, 0, total)
        n = 2 + mu
        from_above = send_down(mu - 1, two_rows(link(mu, 0)))
        new_loop = lower(mu, 0, 0)
        below = send_up(n, new_loop)
        total = plus(both(mu, others[0], 1), both(mu, others[1], 1))
        from_above.wait_recv()
        value = down_in[mu - 1]
        ahead_rows = (roll(value, 1, 2), value)
        below.wait_recv()
        total = plus(total, time_part(mu, 1, ahead_rows, new_loop, n))
        renew(mu, 1, total)
        write(mu)

    for copy in messages:
        copy.wait_send()
    for copy in stores:
        copy.wait()


def on_device(counts, raw_links):
    ta_n, gz_n = counts
    t_len, z_len, lanes = raw_links.shape[4:]
    assert t_len == 2 and z_len % 2 == 0 and lanes == LANES
    piece = t_len * z_len
    rows = gz_n * piece
    f32 = jnp.float32
    dma = pltpu.SemaphoreType.DMA
    side = max(gz_n - 1, 1)
    return pl.pallas_call(
        functools.partial(kernel, (ta_n, gz_n, t_len, z_len)),
        out_shape=jax.ShapeDtypeStruct(raw_links.shape, f32),
        in_specs=[pl.BlockSpec(memory_space=pl.ANY)],
        out_specs=pl.BlockSpec(memory_space=pl.ANY),
        scratch_shapes=[
            pltpu.VMEM((2, 2, 3, 2, 2 * piece, LANES), f32),
            pltpu.VMEM((2, 2, 3, 2, 2 * piece, LANES), f32),
            pltpu.VMEM((2, 4, 2, 3, 2, rows, LANES), f32),
            pltpu.VMEM((2, 3, 2, 3, 2, rows, LANES), f32),
            pltpu.VMEM((2, 4, 3, 3, rows, LANES), f32),
            pltpu.VMEM((2, 4, 3, 3, rows, LANES), f32),
            pltpu.VMEM((2, 3, 3, 3, rows, LANES), f32),
            pltpu.VMEM((2, 3, 3, 3, rows, LANES), f32),
            pltpu.VMEM((6, 2, 3, rows, LANES), f32),
            pltpu.VMEM((6, 2, 3, rows, LANES), f32),
            pltpu.VMEM((3, 2, 3, rows, LANES), f32),
            pltpu.VMEM((3, 2, 3, rows, LANES), f32),
            pltpu.VMEM((4, 3, 3, 2, rows, LANES), f32),
            dma((2 * piece,)),
            dma((4,)),
            dma((4,)),
            dma((4,)),
            dma((side, 4)),
            dma((side, 4)),
            dma((side, 4)),
            dma((side, 4)),
            dma((gz_n, z_len, 3)),
            dma((gz_n, z_len, 3)),
            dma((gz_n, z_len, 3)),
            dma((gz_n, z_len, 3)),
            dma((6,)),
            dma((6,)),
            dma((3,)),
            dma((3,)),
            dma((4, piece)),
        ],
        compiler_params=pltpu.CompilerParams(
            collective_id=0, has_side_effects=True, vmem_limit_bytes=32 * 1024 * 1024
        ),
    )(raw_links)


def solution(mesh):
    spec = P("ens", None, None, None, "ta", "gz", "gy")
    assert mesh.shape["gy"] == 2
    return jax.shard_map(
        functools.partial(on_device, (mesh.shape["ta"], mesh.shape["gz"])),
        mesh=mesh,
        in_specs=(spec,),
        out_specs=spec,
        check_vma=False,
    )
```

```python
import functools

import jax
import jax.numpy as jnp
from jax import lax
from jax.experimental import pallas as pl
from jax.experimental.pallas import tpu as pltpu
from jax.sharding import PartitionSpec as P

X = 16
LANES = 128
MESH = pl.DeviceIdType.MESH


def product(a, b, a_dagger=False, b_dagger=False):
    depth = a[0].shape[0] if a_dagger else a[0].shape[1]
    real = imag = None
    for k in range(depth):
        left = [(part[k] if a_dagger else part[:, k])[:, None] for part in a]
        right = [(part[:, k] if b_dagger else part[k])[None] for part in b]
        if a_dagger != b_dagger:
            real_term = left[0] * right[0] + left[1] * right[1]
            if a_dagger:
                imag_term = left[0] * right[1] - left[1] * right[0]
            else:
                imag_term = left[1] * right[0] - left[0] * right[1]
        else:
            real_term = left[0] * right[0] - left[1] * right[1]
            imag_term = left[0] * right[1] + left[1] * right[0]
        real = real_term if real is None else real + real_term
        imag = imag_term if imag is None else imag + imag_term
    return real, imag


def third(real, imag):
    rows = []
    for j in range(3):
        k, m = (j + 1) % 3, (j + 2) % 3
        a_r, a_i, b_r, b_i = real[0, k], imag[0, k], real[1, m], imag[1, m]
        c_r, c_i, d_r, d_i = real[0, m], imag[0, m], real[1, k], imag[1, k]
        rows.append(
            (
                (a_r * b_r - a_i * b_i) - (c_r * d_r - c_i * d_i),
                (c_r * d_i + c_i * d_r) - (a_r * b_i + a_i * b_r),
            )
        )
    return jnp.stack([r for r, _ in rows]), jnp.stack([i for _, i in rows])


def closed(pair):
    real, imag = pair
    last_r, last_i = third(real, imag)
    return (
        jnp.concatenate([real, last_r[None]], axis=0),
        jnp.concatenate([imag, last_i[None]], axis=0),
    )


def two_rows(pair):
    return pair[0][:2], pair[1][:2]


def two_columns(pair):
    return pair[0][:, :2], pair[1][:, :2]


def plus(a, b):
    return a[0] + b[0], a[1] + b[1]


def roll(value, shift, axis):
    return pltpu.roll(value, shift % value.shape[axis], axis)


def project(rows):
    lead, second = rows[0], rows[1]
    square = lead * lead
    norm = square[0, 0] + square[0, 1] + square[1, 0] + square[1, 1] + square[2, 0] + square[2, 1]
    lead = lead * (1.0 / jnp.sqrt(norm))[None, None]
    cr = ci = None
    for j in range(3):
        r = lead[j, 0] * second[j, 0] + lead[j, 1] * second[j, 1]
        i = lead[j, 0] * second[j, 1] - lead[j, 1] * second[j, 0]
        cr = r if cr is None else cr + r
        ci = i if ci is None else ci + i
    new = []
    norm = None
    for j in range(3):
        r = second[j, 0] - (cr * lead[j, 0] - ci * lead[j, 1])
        i = second[j, 1] - (cr * lead[j, 1] + ci * lead[j, 0])
        new.append((r, i))
        norm = r * r + i * i if norm is None else norm + (r * r + i * i)
    inverse = 1.0 / jnp.sqrt(norm)
    lead = [(lead[j, 0], lead[j, 1]) for j in range(3)]
    return [lead, [(r * inverse, i * inverse) for r, i in new]]


def reflect(link, staple):
    w_r, w_i = product(link, staple)
    w = {(i, j): (w_r[i, j], w_i[i, j]) for i in range(3) for j in range(3)}
    u = {i: (link[0][i], link[1][i]) for i in range(3)}
    needed = {(0, 1): ((0, 1, 2), (1, 2)), (0, 2): ((), (1, 2)), (1, 2): ((), ())}
    for a, b in ((0, 1), (0, 2), (1, 2)):
        q0 = 0.5 * (w[a, a][0] + w[b, b][0])
        q1 = 0.5 * (w[a, b][1] + w[b, a][1])
        q2 = 0.5 * (w[a, b][0] - w[b, a][0])
        q3 = 0.5 * (w[a, a][1] - w[b, b][1])
        vector = q1 * q1 + q2 * q2 + q3 * q3
        square = q0 * q0
        inverse = 1.0 / (square + vector)
        c0 = (square - vector) * inverse
        scale = -2.0 * q0 * inverse
        c1, c2, c3 = scale * q1, scale * q2, scale * q3

        def first(top, low):
            return (
                (c0 * top[0] - c3 * top[1]) + (c2 * low[0] - c1 * low[1]),
                (c0 * top[1] + c3 * top[0]) + (c2 * low[1] + c1 * low[0]),
            )

        def last(top, low):
            return (
                (c0 * low[0] + c3 * low[1]) - (c2 * top[0] + c1 * top[1]),
                (c0 * low[1] - c3 * low[0]) + (c1 * top[0] - c2 * top[1]),
            )

        u[a], u[b] = first(u[a], u[b]), last(u[a], u[b])
        tops, lows = needed[a, b]
        new = {(a, j): first(w[a, j], w[b, j]) for j in tops}
        new.update({(b, j): last(w[a, j], w[b, j]) for j in lows})
        w.update(new)
    return jnp.stack([u[i][0] for i in range(3)]), jnp.stack([u[i][1] for i in range(3)])


def kernel(
    counts,
    x_ref,
    o_ref,
    raw,
    packed,
    edging,
    gathered,
    rim,
    link_r,
    link_i,
    rim_r,
    rim_i,
    up_out,
    up_in,
    down_out,
    down_in,
    natural,
    load_sem,
    own_sem,
    sib_send,
    sib_recv,
    gz_send,
    gz_recv,
    fwd_send,
    fwd_recv,
    rim_send,
    rim_recv,
    rfw_send,
    rfw_recv,
    up_send,
    up_recv,
    down_send,
    down_recv,
    store_sem,
):
    ta_n, gz_n, t_len, z_len = counts
    piece = t_len * z_len
    rows = gz_n * piece
    ta, gz, gy = lax.axis_index("ta"), lax.axis_index("gz"), lax.axis_index("gy")
    later, earlier = lax.rem(ta + 1, ta_n), lax.rem(ta + ta_n - 1, ta_n)
    sibling = {"gy": 1 - gy}

    def side(k):
        return lax.rem(gz + k, gz_n)

    def behind(k):
        return lax.rem(gz + gz_n - k, gz_n)

    loads = []
    for half in range(2):
        for z in range(z_len):
            for t in range(t_len):
                row = half * piece + z * t_len + t
                loads.append(
                    pltpu.make_async_copy(
                        x_ref.at[2 * half : 2 * half + 2, 0:2, :, :, t, z, :],
                        raw.at[:, :, :, :, row, :],
                        load_sem.at[row],
                    )
                )
    for copy in loads:
        copy.start()

    barrier = pltpu.get_barrier_semaphore()
    greeted = [sibling] + [{"gz": side(k)} for k in range(1, gz_n)]
    for k in range(gz_n):
        greeted.append({"ta": later, "gz": side(k)})
        greeted.append({"ta": earlier, "gz": side(k)})
    for device in greeted:
        pl.semaphore_signal(barrier, inc=1, device_id=device, device_id_type=MESH)

    for copy in loads:
        copy.wait()

    small = (2 * piece, LANES)
    row_id = lax.broadcasted_iota(jnp.int32, small, 0)
    lane_id = lax.broadcasted_iota(jnp.int32, small, 1)
    inner = row_id % piece
    place = lane_id % 64
    odd = (inner // t_len + inner % t_len + place // 8 + lane_id // 64) % 2
    pick = (place // 8) * X + 2 * (place % 8) + odd
    for pair in range(2):
        for i, row in enumerate(project(raw[pair])):
            for j, entry in enumerate(row):
                for c in range(2):
                    packed[pair, i, j, c] = jnp.take_along_axis(entry[c], pick, axis=1)

    early_row = row_id % t_len == 0
    for pair in range(2):
        for i in range(2):
            for j in range(3):
                real, imag = packed[pair, i, j, 0], packed[pair, i, j, 1]
                edging[0, pair, i, j] = jnp.where(early_row, real, roll(imag, 1, 0))
                edging[1, pair, i, j] = jnp.where(early_row, roll(real, -1, 0), imag)

    pl.semaphore_wait(barrier, len(greeted))

    def block(half):
        return packed.at[:, :, :, :, pl.ds(half * piece, piece), :]

    def slot(core, half, where):
        return gathered.at[core, 2 * half : 2 * half + 2, :, :, :, pl.ds(where * piece, piece), :]

    def remote(src, dst, send, recv, device):
        return pltpu.make_async_remote_copy(
            src_ref=src, dst_ref=dst, send_sem=send, recv_sem=recv, device_id=device, device_id_type=MESH
        )

    def edge_slot(side_of, half, core, where):
        first = 1 if side_of == 0 and half == 0 else 2 * half
        return rim.at[core, side_of, first : 2 * half + 2, :, :, pl.ds(where * piece, piece), :]

    halves = (0, 1)
    own, near, sent, edge = {}, {}, {}, {}
    for half in halves:
        for k in range(1, gz_n):
            copy = remote(
                block(half),
                slot(gy, half, gz),
                gz_send.at[k - 1, half],
                gz_recv.at[k - 1, half],
                {"gz": side(k)},
            )
            copy.start()
            sent[half, k] = copy
    edges = [(k, side_of, half) for k in reversed(range(gz_n)) for side_of in range(2) for half in halves]
    for k, side_of, half in edges:
        first = 1 if side_of == 0 and half == 0 else 0
        copy = remote(
            edging.at[side_of, first:2, :, :, pl.ds(half * piece, piece), :],
            edge_slot(side_of, half, gy, gz),
            rim_send.at[k, side_of, half],
            rim_recv.at[k, side_of, half],
            {"ta": later if side_of else earlier, "gz": side(k)},
        )
        copy.start()
        edge[k, side_of, half] = copy
    for half in halves:
        near[half] = remote(block(half), slot(gy, half, gz), sib_send.at[half], sib_recv.at[half], sibling)
        near[half].start()
        own[half] = pltpu.make_async_copy(block(half), slot(gy, half, gz), own_sem.at[half])
        own[half].start()
    passed, passed_edges = [], []
    for half in halves:
        for k in range(1, gz_n):
            sent[half, k].wait_recv()
            region = slot(gy, half, behind(k))
            copy = remote(region, region, fwd_send.at[k - 1, half], fwd_recv.at[k - 1, half], sibling)
            copy.start()
            passed.append(copy)

    def pass_edges():
        for k, side_of, half in reversed(edges):
            edge[k, side_of, half].wait_recv()
            region = edge_slot(side_of, half, gy, behind(k))
            copy = remote(
                region,
                region,
                rfw_send.at[k, side_of, half],
                rfw_recv.at[k, side_of, half],
                sibling,
            )
            copy.start()
            passed_edges.append(copy)

    full = (rows, LANES)
    row_id = lax.broadcasted_iota(jnp.int32, full, 0)
    lane_id = lax.broadcasted_iota(jnp.int32, full, 1)
    t_pos = row_id % t_len
    first_t, last_t = t_pos == 0, t_pos == t_len - 1
    low = lane_id < 64
    shade = (row_id // t_len + t_pos + lane_id // 8) % 2
    even_x = (shade == 0, shade == 1)
    x_first, x_last = lane_id % 8 == 0, lane_id % 8 == 7

    def choose(mask, a, b):
        shape = a.shape
        return jnp.where(jnp.broadcast_to(mask, shape), a, b)

    def spread(piece_0, piece_1, put):
        for parity in range(2):
            if parity == 0:
                value = choose(low, piece_0, roll(piece_1, 64, 4))
            else:
                value = choose(low, roll(piece_0, 64, 4), piece_1)
            put(parity, closed((value[:, :, 0], value[:, :, 1])))

    for half in halves:
        own[half].wait()
        near[half].wait()
        for k in range(1, gz_n):
            sent[half, k].wait_send()
    for copy in passed:
        copy.wait()
    for d in range(4):

        def put(parity, pair):
            link_r[0, parity, d], link_i[0, parity, d] = pair

        spread(gathered[0, d], gathered[1, d], put)
    def unfolded(value):
        return jnp.stack([roll(value, 1, 2), value], axis=2)

    pass_edges()
    for copy in edge.values():
        copy.wait_send()
    for copy in passed_edges:
        copy.wait()
    for d in range(1, 4):

        def put(parity, pair):
            rim_r[parity, d - 1], rim_i[parity, d - 1] = pair

        spread(unfolded(rim[0, 0, d]), unfolded(rim[1, 0, d]), put)
    for d in range(4):

        def put(parity, pair):
            link_r[1, parity, d], link_i[1, parity, d] = pair

        spread(unfolded(rim[0, 1, d]), unfolded(rim[1, 1, d]), put)

    def link(d, parity, at=0):
        return link_r[at, parity, d], link_i[at, parity, d]

    def rim_link(d, parity):
        return rim_r[parity, d - 1], rim_i[parity, d - 1]

    def moved(value, direction, sign, parity):
        sub, lane = value.ndim - 2, value.ndim - 1
        if direction == 0:
            return roll(value, -sign, sub)
        if direction == 1:
            return roll(value, -sign * t_len, sub)
        if direction == 2:
            return roll(value, -sign * 8, lane)
        edge_x = x_last if sign > 0 else x_first
        turned = choose(edge_x, roll(value, sign * 7, lane), roll(value, -sign, lane))
        stays = even_x[parity] if sign > 0 else even_x[1 - parity]
        return choose(stays, value, turned)

    def shifted(pair, direction, sign, parity, beyond=None):
        out = []
        for n in range(2):
            value = moved(pair[n], direction, sign, parity)
            if direction == 0:
                value = choose(last_t if sign > 0 else first_t, beyond[n], value)
            out.append(value)
        return tuple(out)

    def ahead(nu, mu, parity, cut, at):
        beyond = None
        if mu == 0 and at == 0:
            beyond = cut(rim_link(nu, 1 - parity))
        elif mu == 0:
            beyond = tuple(roll(part, 1, 2) for part in cut(link(nu, 1 - parity)))
        return shifted(cut(link(nu, 1 - parity, at)), mu, 1, parity, beyond)

    def upper(mu, nu, parity, at=0, beyond=None):
        if nu == 0:
            across = closed(shifted(two_rows(link(mu, 1 - parity)), 0, 1, parity, beyond))
        else:
            across = shifted(link(mu, 1 - parity, at), nu, 1, parity)
        part = product(ahead(nu, mu, parity, two_rows, at), across, b_dagger=True)
        return product(part, link(nu, parity, at), b_dagger=True)

    def lower(mu, nu, parity, at=0):
        part = product(link(mu, parity, at), ahead(nu, mu, parity, two_columns, at))
        return product(part, link(nu, parity, at), a_dagger=True)

    def both(mu, nu, parity, at=0):
        up = closed(upper(mu, nu, parity, at))
        down = closed(shifted(lower(mu, nu, 1 - parity, at), nu, -1, parity))
        return plus(up, down)

    def renew(mu, parity, staple, at=0):
        new = reflect(link(mu, parity, at), staple)
        link_r[at, parity, mu], link_i[at, parity, mu] = new

    messages = []

    def send_up(n, pair):
        up_out[n] = choose(first_t, roll(pair[0], -1, 2), pair[1])
        copy = remote(up_out.at[n], up_in.at[n], up_send.at[n], up_recv.at[n], {"ta": later})
        copy.start()
        messages.append(copy)
        return copy

    def send_down(n, pair):
        down_out[n] = choose(first_t, pair[0], roll(pair[1], 1, 2))
        copy = remote(down_out.at[n], down_in.at[n], down_send.at[n], down_recv.at[n], {"ta": earlier})
        copy.start()
        messages.append(copy)
        return copy

    stores = []
    row_natural = (row_id // t_len + t_pos + lane_id // X + lane_id % X) % 2
    back = (lane_id // X) * 8 + (lane_id % X) // 2 + 64 * row_natural

    def write(d):
        for i in range(3):
            for j in range(3):
                for c, ref in enumerate((link_r, link_i)):
                    zero = jnp.where(gy == 0, ref[0, 0, d, i, j], roll(ref[0, 0, d, i, j], 64, 1))
                    one = jnp.where(gy == 0, roll(ref[0, 1, d, i, j], 64, 1), ref[0, 1, d, i, j])
                    natural[d, i, j, c] = jnp.take_along_axis(jnp.where(low, zero, one), back, axis=1)
        for z in range(z_len):
            for t in range(t_len):
                copy = pltpu.make_async_copy(
                    natural.at[d, :, :, :, gz * piece + z * t_len + t, :],
                    o_ref.at[d, :, :, :, t, z, :],
                    store_sem.at[d, z * t_len + t],
                )
                copy.start()
                stores.append(copy)

    for parity in range(2):
        for at in range(2):
            total = both(0, 1, parity, at)
            for nu in (2, 3):
                total = plus(total, both(0, nu, parity, at))
            renew(0, parity, total, at)

    def upward(pair):
        return tuple(roll(part, -1, 2) for part in pair)

    def time_part(mu, parity, ahead_rows, behind_loop, beyond):
        up = closed(upper(mu, 0, parity, 0, ahead_rows))
        down = closed(shifted(behind_loop, 0, -1, parity, beyond))
        return plus(up, down)

    def time_start(mu):
        return time_part(mu, 0, two_rows(rim_link(mu, 1)), lower(mu, 0, 1), upward(lower(mu, 0, 1, 1)))

    total = plus(plus(both(1, 2, 0), both(1, 3, 0)), time_start(1))
    for mu in (1, 2, 3):
        others = [nu for nu in (1, 2, 3) if nu != mu]
        renew(mu, 0, total)
        from_above = send_down(mu - 1, two_rows(link(mu, 0)))
        new_loop = lower(mu, 0, 0)
        below = send_up(mu - 1, new_loop)
        total = plus(both(mu, others[0], 1), both(mu, others[1], 1))
        if mu == 1:
            write(0)
            early = {2: plus(both(2, 3, 0), time_start(2)), 3: time_start(3)}
        if mu == 2:
            write(1)
            early[3] = plus(early[3], both(3, 1, 0))
        if mu == 3:
            write(2)
        from_above.wait_recv()
        value = down_in[mu - 1]
        ahead_rows = (roll(value, 1, 2), value)
        below.wait_recv()
        value = up_in[mu - 1]
        total = plus(total, time_part(mu, 1, ahead_rows, new_loop, (value, roll(value, -1, 2))))
        renew(mu, 1, total)
        if mu < 3:
            total = plus(early[mu + 1], both(mu + 1, mu, 0))
    write(3)

    for copy in messages:
        copy.wait_send()
    for copy in stores:
        copy.wait()


def on_device(counts, raw_links):
    ta_n, gz_n = counts
    t_len, z_len, lanes = raw_links.shape[4:]
    assert t_len == 2 and z_len % 2 == 0 and lanes == LANES
    piece = t_len * z_len
    rows = gz_n * piece
    f32 = jnp.float32
    dma = pltpu.SemaphoreType.DMA
    side = max(gz_n - 1, 1)
    return pl.pallas_call(
        functools.partial(kernel, (ta_n, gz_n, t_len, z_len)),
        out_shape=jax.ShapeDtypeStruct(raw_links.shape, f32),
        in_specs=[pl.BlockSpec(memory_space=pltpu.HBM)],
        out_specs=pl.BlockSpec(memory_space=pl.ANY),
        scratch_shapes=[
            pltpu.VMEM((2, 2, 3, 2, 2 * piece, LANES), f32),
            pltpu.VMEM((2, 2, 3, 2, 2 * piece, LANES), f32),
            pltpu.VMEM((2, 2, 2, 3, 2 * piece, LANES), f32),
            pltpu.VMEM((2, 4, 2, 3, 2, rows, LANES), f32),
            pltpu.VMEM((2, 2, 4, 2, 3, rows, LANES), f32),
            pltpu.VMEM((2, 2, 4, 3, 3, rows, LANES), f32),
            pltpu.VMEM((2, 2, 4, 3, 3, rows, LANES), f32),
            pltpu.VMEM((2, 3, 3, 3, rows, LANES), f32),
            pltpu.VMEM((2, 3, 3, 3, rows, LANES), f32),
            pltpu.VMEM((3, 2, 3, rows, LANES), f32),
            pltpu.VMEM((3, 2, 3, rows, LANES), f32),
            pltpu.VMEM((3, 2, 3, rows, LANES), f32),
            pltpu.VMEM((3, 2, 3, rows, LANES), f32),
            pltpu.VMEM((4, 3, 3, 2, rows, LANES), f32),
            dma((2 * piece,)),
            dma((2,)),
            dma((2,)),
            dma((2,)),
            dma((side, 2)),
            dma((side, 2)),
            dma((side, 2)),
            dma((side, 2)),
            dma((gz_n, 2, 2)),
            dma((gz_n, 2, 2)),
            dma((gz_n, 2, 2)),
            dma((gz_n, 2, 2)),
            dma((3,)),
            dma((3,)),
            dma((3,)),
            dma((3,)),
            dma((4, piece)),
        ],
        compiler_params=pltpu.CompilerParams(
            collective_id=0, has_side_effects=True, vmem_limit_bytes=32 * 1024 * 1024
        ),
    )(raw_links)


def solution(mesh):
    spec = P("ens", None, None, None, "ta", "gz", "gy")
    assert mesh.shape["gy"] == 2
    return jax.shard_map(
        functools.partial(on_device, (mesh.shape["ta"], mesh.shape["gz"])),
        mesh=mesh,
        in_specs=(spec,),
        out_specs=spec,
        check_vma=False,
    )
```
